512 devices in a mesh: rows: 128 (over y, x, z_hi), chan: 4 (over z_lo, core).
Axes of the slice: x: 4, y: 8, z: 8 (z_hi: 4, z_lo: 2; z = z_hi * 2 + z_lo), core: 2. Of those that a mesh axis runs over, the one named last changes fastest.
Arguments:
- field: float32 [64, 1024, 1024], P('chan', 'rows'), may hold values from -6 to 6
- weights: bfloat16 [2, 64, 64, 65536], P(None, None, None, ('rows', 'chan')), may hold values from -0.5 to 0.5
- cotangent: float32 [64, 512, 512], P('chan', 'rows'), may hold values from -6 to 6
Outputs:
- grad_field: bfloat16 [64, 1024, 1024], P('chan', 'rows')
- grad_weights: bfloat16 [2, 64, 64, 65536], P(None, None, None, ('rows', 'chan'))
The draws below stay inside these ranges and needn't reach their ends.
All inputs are finite; a program needn't handle non-finite values.
Results may differ from the reference program's by a relative error of at most 0.0012.
Values sent between devices are 32-bit elements; how exact they have to be, the bound alone decides.
A program may use at most 64 MiB of HBM per device.

```python
import math
import jax
import jax.numpy as jnp
from jax import lax

C = 64
W = 1024
KW = 256
KH = 256
H = 1024
GH = 512
GW = 512
MODES = 65536


def level_of(key, dims, pieces, low, largest):
    factor_of, own = 1.0, jax.random.fold_in(key, 6)
    for dim, parts in pieces:
        draws = jnp.exp(jax.random.uniform(jax.random.fold_in(own, dim), (parts,), jnp.float32, low / len(pieces), largest / len(pieces)))
        factor_of = factor_of * jnp.repeat(draws, dims[dim] // parts).reshape([-1 if axis == dim else 1 for axis in range(len(dims))])
    return factor_of


def noise(rng, shape, deviation, most, split=(), kind=jnp.bfloat16):
    drawn = deviation * jax.random.normal(rng, shape, jnp.float32)
    if split:
        drawn = drawn * level_of(rng, shape, split, -0.22, 0.18)
    return jnp.clip(drawn, -most, most).astype(kind)


def setup_inputs(seed: int = 0) -> dict:
    splits = jax.random.split(jax.random.key(seed), 4)
    field = noise(splits[0], (C, H, W), 1.0, 6.0, ((0, 4), (1, 128)), jnp.float32)
    weights = noise(splits[1], (2, C, C, MODES), (2 * C) ** -0.5, 0.5, ((3, 512),))
    cotangent = noise(splits[2], (C, GH, GW), 1.0, 6.0, ((0, 4), (1, 128)), jnp.float32)
    return {"field": field, "weights": weights, "cotangent": cotangent}


def gelu_slope(values):
    cdf = 0.5 * (1.0 + jax.scipy.special.erf(values * (1.0 / math.sqrt(2.0))))
    pdf = jnp.exp(-0.5 * values * values) * (1.0 / math.sqrt(2.0 * math.pi))
    return cdf + values * pdf

def reference(field, weights, cotangent):
    block = math.gcd(MODES, 1024)
    blocks = MODES // block
    scale_out = 1.0 / math.sqrt(KH * KW)
    spec = jnp.fft.rfft(field, axis=2)[:, :, :KW] * W ** (-0.5)
    spec = jnp.fft.fft(spec, axis=1) * H ** (-0.5)
    fine_index = (jnp.arange(KH) - KH // 2) % H
    coarse_index = (jnp.arange(KH) - KH // 2) % GH
    spec = spec[:, fine_index, :]
    modes = jnp.transpose(spec, (0, 2, 1)).reshape(C, MODES)
    real_x = jnp.real(modes)
    imag_x = jnp.imag(modes)

    def forward_block(index):
        start = index * block
        part_r = lax.dynamic_slice_in_dim(real_x, start, block, 1)
        part_i = lax.dynamic_slice_in_dim(imag_x, start, block, 1)
        piece = lax.dynamic_slice_in_dim(weights, start, block, 3).astype(jnp.float32)
        high = lax.Precision.HIGHEST
        out_r = jnp.einsum('im,iom->om', part_r, piece[0], precision=high) - jnp.einsum('im,iom->om', part_i, piece[1], precision=high)
        out_i = jnp.einsum('im,iom->om', part_r, piece[1], precision=high) + jnp.einsum('im,iom->om', part_i, piece[0], precision=high)
        return jnp.stack([out_r, out_i])
    out_blocks = lax.map(forward_block, jnp.arange(blocks))
    out_modes = jnp.transpose(out_blocks, (1, 2, 0, 3)).reshape(2, C, MODES)
    out_complex = (out_modes[0] + 1j * out_modes[1]).reshape(C, KW, KH)
    padded = jnp.zeros((C, GH, KW), out_complex.dtype).at[:, coarse_index, :].add(jnp.transpose(out_complex, (0, 2, 1)))
    coarse = jnp.fft.ifft(padded, axis=1) * GH
    wide = jnp.zeros((C, GH, GW), coarse.dtype).at[:, :, :KW].set(coarse)
    values = jnp.real(jnp.fft.ifft(wide, axis=2)) * (GW * scale_out)
    grad_v = cotangent * gelu_slope(values)
    grad_z = jnp.fft.fft(grad_v, axis=2)[:, :, :KW] * scale_out
    grad_y = jnp.fft.fft(grad_z, axis=1)[:, coarse_index, :]
    grad_y = jnp.transpose(grad_y, (0, 2, 1)).reshape(C, MODES)
    real_gy = jnp.real(grad_y)
    imag_gy = jnp.imag(grad_y)

    def backward_block(index):
        start = index * block
        part_r = lax.dynamic_slice_in_dim(real_x, start, block, 1)
        part_i = lax.dynamic_slice_in_dim(imag_x, start, block, 1)
        slope_r = lax.dynamic_slice_in_dim(real_gy, start, block, 1)
        slope_i = lax.dynamic_slice_in_dim(imag_gy, start, block, 1)
        piece = lax.dynamic_slice_in_dim(weights, start, block, 3).astype(jnp.float32)
        high = lax.Precision.HIGHEST
        grad_real = part_r[:, None, :] * slope_r[None] + part_i[:, None, :] * slope_i[None]
        grad_imag = part_r[:, None, :] * slope_i[None] - part_i[:, None, :] * slope_r[None]
        back_r = jnp.einsum('iom,om->im', piece[0], slope_r, precision=high) + jnp.einsum('iom,om->im', piece[1], slope_i, precision=high)
        back_i = jnp.einsum('iom,om->im', piece[0], slope_i, precision=high) - jnp.einsum('iom,om->im', piece[1], slope_r, precision=high)
        return (jnp.stack([grad_real, grad_imag]).astype(jnp.bfloat16), jnp.stack([back_r, back_i]))
    grad_blocks, back_blocks = lax.map(backward_block, jnp.arange(blocks))
    grad_weights = jnp.transpose(grad_blocks, (1, 2, 3, 0, 4)).reshape(2, C, C, MODES)
    back_modes = jnp.transpose(back_blocks, (1, 2, 0, 3)).reshape(2, C, MODES)
    back_complex = (back_modes[0] + 1j * back_modes[1]).reshape(C, KW, KH)
    tall = jnp.zeros((C, H, KW), back_complex.dtype).at[:, fine_index, :].add(jnp.transpose(back_complex, (0, 2, 1)))
    grad_spec = jnp.fft.ifft(tall, axis=1) * (H * H ** (-0.5))
    full = jnp.zeros((C, H, W), grad_spec.dtype).at[:, :, :KW].set(grad_spec)
    grad_field = jnp.real(jnp.fft.ifft(full, axis=2)) * (W * W ** (-0.5))
    return (grad_field.astype(jnp.bfloat16), grad_weights)
```

```python
import functools
import math

import jax
import jax.numpy as jnp
import ml_dtypes
import numpy as np
from jax import lax
from jax.experimental import pallas as pl
from jax.experimental.pallas import tpu as pltpu
from jax.sharding import PartitionSpec as P

MESH = pl.DeviceIdType.MESH
ROWS = 128
CHANS = 4
KW = 256
KH = 256
W = 1024
H = 1024
GH = 512
GW = 512
HL = H // ROWS
TL = GH // ROWS
FAR_FIRST = sorted(
    ((dy, dx, dz) for dx in (2, 1, 3, 0) for dz in (2, 1, 3, 0) for dy in (4, 3, 5, 2, 6, 1, 7, 0) if (dy, dx, dz) != (0, 0, 0)),
    key=lambda o: -(min(o[0], 8 - o[0]) + min(o[1], 4 - o[1]) + 2 * min(o[2], 4 - o[2])),
)
NT = (((1,), (1,)), ((), ()))
NN = (((1,), (0,)), ((), ()))


def split_table(table):
    high = table.astype(np.float32).astype(ml_dtypes.bfloat16)
    low = (table - high.astype(np.float64)).astype(np.float32).astype(ml_dtypes.bfloat16)
    return high, low


def wave(first, second, length):
    angle = (first[:, None] * second[None, :]) % length * (2.0 * math.pi / length)
    return np.cos(angle), np.sin(angle)


def tables():
    dev = np.arange(ROWS)
    freq = np.arange(KH) - KH // 2
    fine, coarse = [], []
    for k in range(2):
        c, s = wave(2 * dev + k, np.arange(W), W)
        fine += [c / math.sqrt(W), -s / math.sqrt(W)]
        c, s = wave(2 * dev + k, np.arange(GW), GW)
        coarse += [c / math.sqrt(KH * KW), -s / math.sqrt(KH * KW)]
    tall, short = [], []
    for h in range(HL):
        c, s = wave(HL * dev + h, freq, H)
        tall.append(np.concatenate([c, s], 1) / math.sqrt(H))
    for t in range(TL):
        c, s = wave(TL * dev + t, freq, GH)
        short.append(np.concatenate([c, s], 1))
    out = []
    for parts in (fine, tall, short, coarse):
        out += split_table(np.concatenate(parts, 0))
    return out


def halves(value):
    high = value.astype(jnp.bfloat16)
    return high, (value - high.astype(jnp.float32)).astype(jnp.bfloat16)


def dot3(a, b, dims):
    def one(x, y):
        return lax.dot_general(x, y, dims, preferred_element_type=jnp.float32)

    return one(a[0], b[1]) + one(a[1], b[0]) + one(a[0], b[0])


def gelu_slope(values):
    cdf = 0.5 * (1.0 + lax.erf(values * (1.0 / math.sqrt(2.0))))
    pdf = jnp.exp(-0.5 * values * values) * (1.0 / math.sqrt(2.0 * math.pi))
    return cdf + values * pdf


def kernel(
    field_hbm, weights_hbm, cot_hbm, fine_h, fine_l, tall_h, tall_l, short_h, short_l, coarse_h, coarse_l,
    gfield_hbm, gweights_hbm,
    field, weights, cot, t1h, t1l, t2h, t2l, t3h, t3l, t4h, t4l, gfield, gweights,
    send1, recv1, send2, recv2, send3, recv3, send4, recv4,
    csend, crecv, turned, mixed, modes_r, modes_i, slope_r, slope_i, back_r, back_i,
    in_sem, out_sem, row_send, row_recv, chan_send, chan_recv,
):
    me = lax.axis_index("rows")
    mc = lax.axis_index("chan")
    me_y, me_x, me_z = me // 16, lax.rem(me // 4, 4), lax.rem(me, 4)

    barrier = pltpu.get_barrier_semaphore()

    def greet(k, _):
        pl.semaphore_signal(barrier, inc=1, device_id={"rows": lax.rem(me + k, ROWS)}, device_id_type=MESH)
        return 0

    lax.fori_loop(1, ROWS, greet, 0, unroll=8)
    for k in range(1, CHANS):
        pl.semaphore_signal(barrier, inc=1, device_id={"chan": lax.rem(mc + k, CHANS)}, device_id_type=MESH)

    loads = [
        pltpu.make_async_copy(src, dst, in_sem.at[n])
        for n, (src, dst) in enumerate(
            [
                (field_hbm, field), (fine_h, t1h), (fine_l, t1l), (tall_h, t2h), (tall_l, t2l),
                (weights_hbm, weights), (short_h, t3h), (short_l, t3l), (coarse_h, t4h), (coarse_l, t4l),
                (cot_hbm, cot),
            ]
        )
    ]
    for load in loads:
        load.start()

    def spread_rows(send, recv, n):
        for dy, dx, dz in FAR_FIRST:
            d = lax.rem(me_y + dy, 8) * 16 + lax.rem(me_x + dx, 4) * 4 + lax.rem(me_z + dz, 4)
            pltpu.make_async_remote_copy(
                src_ref=send.at[d], dst_ref=recv.at[me], send_sem=row_send.at[n], recv_sem=row_recv.at[n],
                device_id={"rows": d}, device_id_type=MESH,
            ).start()
        recv[me] = send[me]

    def await_rows(recv, n):
        part = recv.at[pl.ds(0, ROWS - 1)]
        pltpu.make_async_copy(part, part, row_recv.at[n]).wait()

    def spread_chans(n):
        for k in range(1, CHANS):
            d = lax.rem(mc + k, CHANS)
            pltpu.make_async_remote_copy(
                src_ref=csend.at[n, d], dst_ref=crecv.at[n, mc], send_sem=chan_send.at[n], recv_sem=chan_recv.at[n],
                device_id={"chan": d}, device_id_type=MESH,
            ).start()
        crecv[n, mc] = csend[n, mc]

    def await_chans(n):
        part = crecv.at[n, pl.ds(0, CHANS - 1)]
        pltpu.make_async_copy(part, part, chan_recv.at[n]).wait()

    def to_modes(product, n):
        for k in range(2):
            re, im = product[32 * k : 32 * k + 16], product[32 * k + 16 : 32 * k + 32]
            real = re[:, :KH] + im[:, KH:]
            imag = im[:, :KH] - re[:, KH:]
            for j in range(2):
                csend[n, 2 * k + j, 0:16, :] = real[:, 128 * j : 128 * j + 128]
                csend[n, 2 * k + j, 16:32, :] = imag[:, 128 * j : 128 * j + 128]
        spread_chans(n)

    def own_modes(n, real, imag):
        for s in range(CHANS):
            real[16 * s : 16 * s + 16, :] = crecv[n, s, 0:16, :]
            imag[16 * s : 16 * s + 16, :] = crecv[n, s, 16:32, :]

    def from_modes(n):
        rows = []
        for k in range(2):
            real = jnp.concatenate([crecv[n, 2 * k, 0:16, :], crecv[n, 2 * k + 1, 0:16, :]], axis=1)
            imag = jnp.concatenate([crecv[n, 2 * k, 16:32, :], crecv[n, 2 * k + 1, 16:32, :]], axis=1)
            rows.append(jnp.concatenate([real, -imag], axis=1))
            rows.append(jnp.concatenate([imag, real], axis=1))
        return halves(jnp.concatenate(rows, axis=0))

    def give_modes(n, real, imag):
        for d in range(CHANS):
            csend[n, d, 0:16, :] = real[16 * d : 16 * d + 16, :]
            csend[n, d, 16:32, :] = imag[16 * d : 16 * d + 16, :]
        spread_chans(n)

    for n in (0, 1, 2):
        loads[n].wait()
    fine = (t1h[...], t1l[...])
    spectra = dot3(fine, halves(field[...]), NT)
    for s in range(4):
        send1[:, s, :] = spectra[128 * s : 128 * s + 128]
    pl.semaphore_wait(barrier, ROWS - 1 + CHANS - 1)
    spread_rows(send1, recv1, 0)
    for n in range(3, 11):
        loads[n].wait()
    await_rows(recv1, 0)

    for s in range(4):
        turned[s] = recv1[:, s, :].T
    left = jnp.concatenate(
        [
            jnp.concatenate([turned[s, pl.ds(h, 16, stride=HL), :] for h in range(HL)], axis=1)
            for s in range(4)
        ],
        axis=0,
    )
    to_modes(dot3(halves(left), (t2h[...], t2l[...]), NN), 0)
    await_chans(0)
    own_modes(0, modes_r, modes_i)

    def mix(i, carry):
        out_r, out_i = carry
        xr, xi = modes_r[pl.ds(i, 1), :], modes_i[pl.ds(i, 1), :]
        wr, wi = weights[0, i].astype(jnp.float32), weights[1, i].astype(jnp.float32)
        return out_r + xr * wr - xi * wi, out_i + xr * wi + xi * wr

    zero = jnp.zeros((64, 128), jnp.float32)
    out_r, out_i = lax.fori_loop(0, 64, mix, (zero, zero), unroll=4)
    give_modes(1, out_r, out_i)
    await_chans(1)

    rows_t = dot3((t3h[...], t3l[...]), from_modes(1), NT)
    for s in range(2):
        send2[:, s, :] = jnp.concatenate([rows_t[256 * s : 256 * s + 128], rows_t[256 * s + 128 : 256 * s + 256]], axis=1)
    spread_rows(send2, recv2, 1)
    await_rows(recv2, 1)
    rows = []
    for s in range(2):
        turn = recv2[:, s, :].T
        for t in range(2):
            rows.append(jnp.concatenate([turn[64 * t + 16 * u : 64 * t + 16 * u + 16] for u in range(4)], axis=1))
    coarse = (t4h[...], t4l[...])
    values = dot3(halves(jnp.concatenate(rows, axis=0)), coarse, NN)
    cotangent = jnp.concatenate([cot[:, t, :] for t in range(TL)], axis=0)
    grad_v = cotangent * gelu_slope(values)

    cols_t = dot3(coarse, halves(grad_v), NT)
    for s in range(2):
        send3[:, s, :] = jnp.concatenate([cols_t[256 * s : 256 * s + 128], cols_t[256 * s + 128 : 256 * s + 256]], axis=1)
    spread_rows(send3, recv3, 2)
    await_rows(recv3, 2)
    rows = []
    for s in range(2):
        turn = recv3[:, s, :].T
        for p in range(2):
            rows.append(jnp.concatenate([turn[64 * p + 16 * u : 64 * p + 16 * u + 16] for u in range(4)], axis=1))
    to_modes(dot3(halves(jnp.concatenate(rows, axis=0)), (t3h[...], t3l[...]), NN), 2)
    await_chans(2)
    own_modes(2, slope_r, slope_i)

    def unmix(i, _):
        gr, gi = slope_r[...], slope_i[...]
        wr, wi = weights[0, i].astype(jnp.float32), weights[1, i].astype(jnp.float32)
        back_r[pl.ds(i, 1), :] = jnp.sum(wr * gr + wi * gi, axis=0, keepdims=True)
        back_i[pl.ds(i, 1), :] = jnp.sum(wr * gi - wi * gr, axis=0, keepdims=True)
        return 0

    lax.fori_loop(0, 64, unmix, 0, unroll=4)
    give_modes(3, back_r, back_i)

    def outer(i, _):
        gr, gi = slope_r[...], slope_i[...]
        xr, xi = modes_r[pl.ds(i, 1), :], modes_i[pl.ds(i, 1), :]
        gweights[0, i] = (xr * gr + xi * gi).astype(jnp.bfloat16)
        gweights[1, i] = (xr * gi - xi * gr).astype(jnp.bfloat16)
        return 0

    await_chans(3)

    fine_t = dot3((t2h[...], t2l[...]), from_modes(3), NT)
    for s in range(4):
        send4[:, s, :] = jnp.concatenate([fine_t[256 * s : 256 * s + 128], fine_t[256 * s + 128 : 256 * s + 256]], axis=1)
    spread_rows(send4, recv4, 3)
    lax.fori_loop(0, 64, outer, 0, unroll=4)
    store = pltpu.make_async_copy(gweights, gweights_hbm, out_sem.at[0])
    store.start()
    await_rows(recv4, 3)
    for s in range(4):
        turn = recv4[:, s, :].T
        for h in range(2):
            for u in range(4):
                mixed[u, pl.ds(2 * s + h, 16, stride=HL), :] = turn[64 * h + 16 * u : 64 * h + 16 * u + 16]
    left = jnp.concatenate([mixed[u] for u in range(4)], axis=1)
    gfield[...] = dot3(halves(left), (t1h[...], t1l[...]), NN)
    last = pltpu.make_async_copy(gfield, gfield_hbm, out_sem.at[1])
    last.start()
    for n, send in enumerate((send1, send2, send3, send4)):
        part = send.at[pl.ds(0, ROWS - 1)]
        pltpu.make_async_copy(part, part, row_send.at[n]).wait()
    for n in range(4):
        part = csend.at[n, pl.ds(0, CHANS - 1)]
        pltpu.make_async_copy(part, part, chan_send.at[n]).wait()
    store.wait()
    last.wait()


def local(field, weights, cotangent):
    consts = [jnp.asarray(t) for t in tables()]
    f32, bf16 = jnp.float32, jnp.bfloat16
    anywhere = pl.BlockSpec(memory_space=pl.ANY)
    gfield, gweights = pl.pallas_call(
        kernel,
        out_shape=(
            jax.ShapeDtypeStruct((128, W), f32),
            jax.ShapeDtypeStruct(weights.shape, bf16),
        ),
        in_specs=[anywhere] * 11,
        out_specs=(anywhere, anywhere),
        scratch_shapes=[
            pltpu.VMEM((128, W), f32),
            pltpu.VMEM(weights.shape, bf16),
            pltpu.VMEM(cotangent.shape, f32),
            *[pltpu.VMEM(t.shape, bf16) for t in consts],
            pltpu.VMEM((128, W), f32),
            pltpu.VMEM(weights.shape, bf16),
            *[pltpu.VMEM((ROWS, n, 128), f32) for n in (4, 4, 2, 2, 2, 2, 4, 4)],
            pltpu.VMEM((4, CHANS, 32, 128), f32),
            pltpu.VMEM((4, CHANS, 32, 128), f32),
            pltpu.VMEM((4, 128, 128), f32),
            pltpu.VMEM((4, 128, 128), f32),
            *[pltpu.VMEM((64, 128), f32)] * 6,
            pltpu.SemaphoreType.DMA((11,)),
            pltpu.SemaphoreType.DMA((2,)),
            pltpu.SemaphoreType.DMA((4,)),
            pltpu.SemaphoreType.DMA((4,)),
            pltpu.SemaphoreType.DMA((4,)),
            pltpu.SemaphoreType.DMA((4,)),
        ],
        compiler_params=pltpu.CompilerParams(
            collective_id=0, has_side_effects=True, vmem_limit_bytes=48 * 2**20
        ),
    )(field.reshape(128, W), weights, cotangent, *consts)
    return gfield.astype(bf16).reshape(field.shape), gweights


def solution(mesh):
    spread = P("chan", "rows", None)
    by_mode = P(None, None, None, ("rows", "chan"))
    return jax.shard_map(
        local, mesh=mesh, in_specs=(spread, by_mode, spread), out_specs=(spread, by_mode), check_vma=False
    )
```

```python
import math

import jax
import jax.numpy as jnp
import ml_dtypes
import numpy as np
from jax import lax
from jax.experimental import pallas as pl
from jax.experimental.pallas import tpu as pltpu
from jax.sharding import PartitionSpec as P

MESH = pl.DeviceIdType.MESH
ROWS = 128
CHANS = 4
KW = 256
KH = 256
W = 1024
H = 1024
GH = 512
GW = 512
HL = H // ROWS
TL = GH // ROWS
FAR_FIRST = sorted(
    ((dy, dx, dz) for dx in (2, 1, 3, 0) for dz in (2, 1, 3, 0) for dy in (4, 3, 5, 2, 6, 1, 7, 0) if (dy, dx, dz) != (0, 0, 0)),
    key=lambda o: -(min(o[0], 8 - o[0]) + min(o[1], 4 - o[1]) + 2 * min(o[2], 4 - o[2])),
)
NT = (((1,), (1,)), ((), ()))
NN = (((1,), (0,)), ((), ()))


def split_table(table):
    high = table.astype(np.float32).astype(ml_dtypes.bfloat16)
    low = (table - high.astype(np.float64)).astype(np.float32).astype(ml_dtypes.bfloat16)
    return high, low


def wave(first, second, length):
    angle = (first[:, None] * second[None, :]) % length * (2.0 * math.pi / length)
    return np.cos(angle), np.sin(angle)


def tables():
    dev = np.arange(ROWS)
    freq = np.arange(KH) - KH // 2
    fine, coarse = [], []
    for k in range(2):
        c, s = wave(2 * dev + k, np.arange(W // 2), W)
        fine += [c / math.sqrt(W), -s / math.sqrt(W)]
        c, s = wave(2 * dev + k, np.arange(GW // 2), GW)
        coarse += [c / math.sqrt(KH * KW), -s / math.sqrt(KH * KW)]
    c, s = wave(dev, dev, ROWS)
    ahead = np.block([[c, -s], [s, c]])
    back = np.concatenate([c, s], 1)
    out = []
    for table in (np.concatenate(fine, 0), np.concatenate(coarse, 0), ahead, back):
        out += split_table(table)
    twiddle = np.zeros((4, 8, KH))
    twiddle[0], twiddle[1] = (t / math.sqrt(H) for t in wave(np.arange(HL), freq, H))
    twiddle[2, :TL], twiddle[3, :TL] = wave(np.arange(TL), freq, GH)
    return out + [twiddle.astype(np.float32)]


def halves(value):
    high = value.astype(jnp.bfloat16)
    return high, (value - high.astype(jnp.float32)).astype(jnp.bfloat16)


def dot3(a, b, dims):
    def one(x, y):
        return lax.dot_general(x, y, dims, preferred_element_type=jnp.float32)

    return one(a[0], b[1]) + one(a[1], b[0]) + one(a[0], b[0])


def gelu_slope(values):
    cdf = 0.5 * (1.0 + lax.erf(values * (1.0 / math.sqrt(2.0))))
    pdf = jnp.exp(-0.5 * values * values) * (1.0 / math.sqrt(2.0 * math.pi))
    return cdf + values * pdf


def kernel(
    field_hbm, weights_hbm, cot_hbm, fine_h, fine_l, coarse_h, coarse_l, ahead_h, ahead_l, behind_h, behind_l, twiddle_hbm,
    left_h, left_l, t1h, t1l, gweights,
    field, weights, cot, t4h, t4l, wah, wal, wbh, wbl, twiddle,
    send1, recv1, send2, recv2, send3, recv3, send4, recv4,
    csend, crecv, mixed, part_r, part_i, back_r, back_i,
    in_sem, row_send, row_recv, chan_send, chan_recv,
):
    me = lax.axis_index("rows")
    mc = lax.axis_index("chan")
    me_y, me_x, me_z = me // 16, lax.rem(me // 4, 4), lax.rem(me, 4)
    others = [lax.rem(mc + k, CHANS) for k in range(1, CHANS)]

    def partner(offset):
        dy, dx, dz = offset
        return lax.rem(me_y + dy, 8) * 16 + lax.rem(me_x + dx, 4) * 4 + lax.rem(me_z + dz, 4)

    barrier = pltpu.get_barrier_semaphore()
    for offset in FAR_FIRST:
        pl.semaphore_signal(barrier, inc=1, device_id={"rows": partner(offset)}, device_id_type=MESH)
    for d in others:
        pl.semaphore_signal(barrier, inc=1, device_id={"chan": d}, device_id_type=MESH)

    loads = [
        pltpu.make_async_copy(src, dst, in_sem.at[n])
        for n, (src, dst) in enumerate(
            [
                (field_hbm, field), (fine_h, t1h), (fine_l, t1l), (ahead_h, wah), (ahead_l, wal), (twiddle_hbm, twiddle),
                (weights_hbm, weights), (behind_h, wbh), (behind_l, wbl), (coarse_h, t4h), (coarse_l, t4l), (cot_hbm, cot),
            ]
        )
    ]
    for load in loads:
        load.start()

    def spread_rows(send, recv, n):
        for offset in FAR_FIRST:
            d = partner(offset)
            pltpu.make_async_remote_copy(
                src_ref=send.at[d], dst_ref=recv.at[me], send_sem=row_send.at[n], recv_sem=row_recv.at[n],
                device_id={"rows": d}, device_id_type=MESH,
            ).start()
        recv[me] = send[me]

    def await_rows(recv, n):
        part = recv.at[pl.ds(0, ROWS - 1)]
        pltpu.make_async_copy(part, part, row_recv.at[n]).wait()

    def spread_chans(n):
        for d in others:
            pltpu.make_async_remote_copy(
                src_ref=csend.at[n, d], dst_ref=crecv.at[n, mc], send_sem=chan_send.at[n], recv_sem=chan_recv.at[n],
                device_id={"chan": d}, device_id_type=MESH,
            ).start()
        crecv[n, mc] = csend[n, mc]

    def await_chans(n):
        part = crecv.at[n, pl.ds(0, CHANS - 1)]
        pltpu.make_async_copy(part, part, chan_recv.at[n]).wait()

    def to_modes(rows, steps, table, n):
        product = dot3(halves(rows), (wah[...], wal[...]), NN)
        for k in range(2):
            for j in range(2):
                lanes = slice(128 * j, 128 * j + 128)
                real = imag = None
                for l in range(steps):
                    first = 16 * (steps * k + l)
                    re, im = product[first : first + 16, :128], product[first : first + 16, 128:]
                    c, s = twiddle[table, l : l + 1, lanes], twiddle[table + 1, l : l + 1, lanes]
                    more_r, more_i = c * re + s * im, c * im - s * re
                    real, imag = (more_r, more_i) if l == 0 else (real + more_r, imag + more_i)
                csend[n, 2 * k + j, 0:16, :] = real
                csend[n, 2 * k + j, 16:32, :] = imag
        spread_chans(n)

    def from_modes(n, steps, table):
        rows = []
        for l in range(steps):
            for k in range(2):
                real = imag = 0.0
                for j in range(2):
                    lanes = slice(128 * j, 128 * j + 128)
                    re, im = crecv[n, 2 * k + j, 0:16, :], crecv[n, 2 * k + j, 16:32, :]
                    c, s = twiddle[table, l : l + 1, lanes], twiddle[table + 1, l : l + 1, lanes]
                    real, imag = real + (c * re - s * im), imag + (s * re + c * im)
                rows.append(jnp.concatenate([real, -imag], axis=1))
                rows.append(jnp.concatenate([imag, real], axis=1))
        return dot3((wbh[...], wbl[...]), halves(jnp.concatenate(rows, axis=0)), NT)

    def give_modes(n, real, imag):
        for d in range(CHANS):
            csend[n, d, 0:16, :] = real[16 * d : 16 * d + 16, :]
            csend[n, d, 16:32, :] = imag[16 * d : 16 * d + 16, :]
        spread_chans(n)

    for n in (0, 1, 2):
        loads[n].wait()
    lines = jnp.concatenate([field[:, l, :] for l in range(HL)], axis=0)
    for k, folded in enumerate((lines[:, : W // 2] + lines[:, W // 2 :], lines[:, : W // 2] - lines[:, W // 2 :])):
        table = (t1h[256 * k : 256 * k + 256, :], t1l[256 * k : 256 * k + 256, :])
        spectra = dot3(table, halves(folded), NT)
        send1[:, 2 * k, :] = spectra[:128]
        send1[:, 2 * k + 1, :] = spectra[128:]
    pl.semaphore_wait(barrier, ROWS - 1 + CHANS - 1)
    spread_rows(send1, recv1, 0)
    for n in range(3, 12):
        loads[n].wait()
    await_rows(recv1, 0)

    rows = [jnp.concatenate([recv1[:, 2 * k, :].T, recv1[:, 2 * k + 1, :].T], axis=1) for k in range(2)]
    to_modes(jnp.concatenate(rows, axis=0), HL, 0, 0)

    def mix(ref, s, carry):
        def step(i, carry):
            out_r, out_i = carry
            xr, xi = ref[0, s, pl.ds(i, 1), :], ref[0, s, pl.ds(16 + i, 1), :]
            wr, wi = weights[0, 16 * s + i].astype(jnp.float32), weights[1, 16 * s + i].astype(jnp.float32)
            return out_r + (xr * wr - xi * wi), out_i + (xr * wi + xi * wr)

        return lax.fori_loop(0, 16, step, carry, unroll=4)

    zero = jnp.zeros((64, 128), jnp.float32)
    total = mix(csend, mc, (zero, zero))
    await_chans(0)
    for s in others:
        total = mix(crecv, s, total)
    give_modes(1, *total)
    await_chans(1)

    short = from_modes(1, TL, 2)
    for s in range(2):
        send2[:, s, :] = short[:, 128 * s : 128 * s + 128]
    spread_rows(send2, recv2, 1)
    await_rows(recv2, 1)
    turns = [recv2[:, s, :].T for s in range(2)]
    parts = []
    for k in range(2):
        rows = []
        for t in range(TL):
            first = 64 * (t % 2) + 32 * k
            rows.append(jnp.concatenate([turns[t // 2][first : first + 16], turns[t // 2][first + 16 : first + 32]], axis=1))
        table = (t4h[256 * k : 256 * k + 256, :], t4l[256 * k : 256 * k + 256, :])
        parts.append(dot3(halves(jnp.concatenate(rows, axis=0)), table, NN))
    values = jnp.concatenate([parts[0] + parts[1], parts[0] - parts[1]], axis=1)
    cotangent = jnp.concatenate([cot[:, t, :] for t in range(TL)], axis=0)
    grad_v = cotangent * gelu_slope(values)

    for k, folded in enumerate((grad_v[:, :256] + grad_v[:, 256:], grad_v[:, :256] - grad_v[:, 256:])):
        table = (t4h[256 * k : 256 * k + 256, :], t4l[256 * k : 256 * k + 256, :])
        cols = dot3(table, halves(folded), NT)
        send3[:, k, :] = jnp.concatenate([cols[:128], cols[128:]], axis=1)
    spread_rows(send3, recv3, 2)
    await_rows(recv3, 2)
    turns = [recv3[:, k, :].T for k in range(2)]
    rows = [jnp.concatenate([turn[:64], turn[64:]], axis=1) for turn in turns]
    to_modes(jnp.concatenate(rows, axis=0), TL, 2, 2)

    def terms(ref, s, i):
        gr, gi = ref[2, s, 0:16, :], ref[2, s, 16:32, :]
        own = pl.ds(pl.multiple_of(16 * s, 16), 16)
        wr, wi = weights[0, i, own, :].astype(jnp.float32), weights[1, i, own, :].astype(jnp.float32)
        real, imag = wr * gr + wi * gi, wr * gi - wi * gr
        return real[:8] + real[8:], imag[:8] + imag[8:]

    def unmix_own(i, _):
        part_r[i], part_i[i] = terms(csend, mc, i)
        return 0

    def unmix(i, _):
        real, imag = part_r[i], part_i[i]
        for s in others:
            more_r, more_i = terms(crecv, s, i)
            real, imag = real + more_r, imag + more_i
        back_r[pl.ds(i, 1), :] = jnp.sum(real, axis=0, keepdims=True)
        back_i[pl.ds(i, 1), :] = jnp.sum(imag, axis=0, keepdims=True)
        return 0

    lax.fori_loop(0, 64, unmix_own, 0, unroll=4)
    await_chans(2)
    lax.fori_loop(0, 64, unmix, 0, unroll=4)
    give_modes(3, back_r, back_i)
    await_chans(3)

    tall = from_modes(3, HL, 0)
    for s in range(4):
        send4[:, s, :] = tall[:, 128 * s : 128 * s + 128]
    spread_rows(send4, recv4, 3)

    def outer(i, _):
        s, c = i // 16, lax.rem(i, 16)
        xr, xi = crecv[0, s, pl.ds(c, 1), :], crecv[0, s, pl.ds(16 + c, 1), :]
        for o in range(CHANS):
            gr, gi = crecv[2, o, 0:16, :], crecv[2, o, 16:32, :]
            gweights[0, i, 16 * o : 16 * o + 16, :] = (xr * gr + xi * gi).astype(jnp.bfloat16)
            gweights[1, i, 16 * o : 16 * o + 16, :] = (xr * gi - xi * gr).astype(jnp.bfloat16)
        return 0

    lax.fori_loop(0, 64, outer, 0, unroll=4)
    for n, send in enumerate((send1, send2, send3)):
        part = send.at[pl.ds(0, ROWS - 1)]
        pltpu.make_async_copy(part, part, row_send.at[n]).wait()
    for n in range(4):
        part = csend.at[n, pl.ds(0, CHANS - 1)]
        pltpu.make_async_copy(part, part, chan_send.at[n]).wait()
    await_rows(recv4, 3)
    for s in range(4):
        turn = recv4[:, s, :].T
        for l in range(2):
            for u in range(4):
                mixed[u, pl.ds(2 * s + l, 16, stride=HL), :] = turn[64 * l + 16 * u : 64 * l + 16 * u + 16]
    for k in range(2):
        high, low = halves(jnp.concatenate([mixed[2 * k], mixed[2 * k + 1]], axis=1))
        left_h[128 * k : 128 * k + 128, :] = high
        left_l[128 * k : 128 * k + 128, :] = low
    part = send4.at[pl.ds(0, ROWS - 1)]
    pltpu.make_async_copy(part, part, row_send.at[3]).wait()


def finish(left_h, left_l, t1h, t1l, gweights, gfield, gweights_hbm, sem):
    store = pltpu.make_async_copy(gweights, gweights_hbm, sem)
    store.start()
    parts = []
    for k in range(2):
        lines, table = slice(128 * k, 128 * k + 128), slice(256 * k, 256 * k + 256)
        parts.append(dot3((left_h[lines, :], left_l[lines, :]), (t1h[table, :], t1l[table, :]), NN))
    whole = jnp.concatenate([parts[0] + parts[1], parts[0] - parts[1]], axis=1)
    gfield[...] = whole.reshape(gfield.shape).astype(jnp.bfloat16)
    store.wait()


def local(field, weights, cotangent):
    f32, bf16 = jnp.float32, jnp.bfloat16
    consts = [jnp.asarray(t) for t in tables()]
    anywhere = pl.BlockSpec(memory_space=pl.ANY)
    inside = pl.BlockSpec(memory_space=pltpu.VMEM)
    operands = [pltpu.with_memory_space_constraint(x, pltpu.HBM) for x in (field, weights, cotangent, *consts)]
    kept = pl.pallas_call(
        kernel,
        out_shape=(
            pltpu.VMEM((256, 256), bf16),
            pltpu.VMEM((256, 256), bf16),
            pltpu.VMEM(consts[0].shape, bf16),
            pltpu.VMEM(consts[1].shape, bf16),
            pltpu.VMEM(weights.shape, bf16),
        ),
        in_specs=[anywhere] * len(operands),
        out_specs=(inside,) * 5,
        scratch_shapes=[
            pltpu.VMEM(field.shape, f32),
            pltpu.VMEM(weights.shape, bf16),
            pltpu.VMEM(cotangent.shape, f32),
            *[pltpu.VMEM(t.shape, t.dtype) for t in consts[2:]],
            *[pltpu.VMEM((ROWS, n, 128), f32) for n in (4, 4, 2, 2, 2, 2, 4, 4)],
            pltpu.VMEM((4, CHANS, 32, 128), f32),
            pltpu.VMEM((4, CHANS, 32, 128), f32),
            pltpu.VMEM((4, 128, 128), f32),
            *[pltpu.VMEM((64, 8, 128), f32)] * 2,
            *[pltpu.VMEM((64, 128), f32)] * 2,
            pltpu.SemaphoreType.DMA((12,)),
            pltpu.SemaphoreType.DMA((4,)),
            pltpu.SemaphoreType.DMA((4,)),
            pltpu.SemaphoreType.DMA((4,)),
            pltpu.SemaphoreType.DMA((4,)),
        ],
        compiler_params=pltpu.CompilerParams(
            collective_id=0, has_side_effects=True, vmem_limit_bytes=40 * 2**20
        ),
    )(*operands)
    return pl.pallas_call(
        finish,
        out_shape=(
            jax.ShapeDtypeStruct(field.shape, bf16),
            jax.ShapeDtypeStruct(weights.shape, bf16),
        ),
        in_specs=[inside] * 5,
        out_specs=(inside, anywhere),
        scratch_shapes=[pltpu.SemaphoreType.DMA],
        compiler_params=pltpu.CompilerParams(vmem_limit_bytes=16 * 2**20),
    )(*kept)


def solution(mesh):
    spread = P("chan", "rows", None)
    by_mode = P(None, None, None, ("rows", "chan"))
    return jax.shard_map(
        local, mesh=mesh, in_specs=(spread, by_mode, spread), out_specs=(spread, by_mode), check_vma=False
    )
```

```python
import math

import jax
import jax.numpy as jnp
import ml_dtypes
import numpy as np
from jax import lax
from jax.experimental import pallas as pl
from jax.experimental.pallas import tpu as pltpu
from jax.sharding import PartitionSpec as P

MESH = pl.DeviceIdType.MESH
ROWS = 128
CHANS = 4
KW = 256
KH = 256
W = 1024
H = 1024
GH = 512
GW = 512
HL = H // ROWS
TL = GH // ROWS
EIGHT = (4, 3, 5, 2, 6, 1, 7, 0)
FAR_FIRST = sorted(
    ((dy, dx, dz) for dx in (2, 1, 3, 0) for dz in EIGHT for dy in EIGHT if (dy, dx, dz) != (0, 0, 0)),
    key=lambda o: -(min(o[0], 8 - o[0]) + min(o[1], 4 - o[1]) + min(o[2], 8 - o[2])),
)
NT = (((1,), (1,)), ((), ()))
NN = (((1,), (0,)), ((), ()))


def split_table(table):
    high = table.astype(np.float32).astype(ml_dtypes.bfloat16)
    low = (table - high.astype(np.float64)).astype(np.float32).astype(ml_dtypes.bfloat16)
    return high, low


def wave(first, second, length):
    angle = (first[:, None] * second[None, :]) % length * (2.0 * math.pi / length)
    return np.cos(angle), np.sin(angle)


def tables():
    dev = np.arange(ROWS)
    freq = np.arange(KH) - KH // 2
    fine, coarse = [], []
    for k in range(2):
        c, s = wave(2 * dev + k, np.arange(W // 2), W)
        fine += [c / math.sqrt(W), -s / math.sqrt(W)]
        c, s = wave(2 * dev + k, np.arange(GW // 2), GW)
        coarse += [c / math.sqrt(KH * KW), -s / math.sqrt(KH * KW)]
    c, s = wave(dev, dev, ROWS)
    ahead = np.block([[c, -s], [s, c]])
    back = np.concatenate([c, s], 1)
    out = []
    for table in (np.concatenate(fine, 0), np.concatenate(coarse, 0), ahead, back):
        out += split_table(table)
    twiddle = np.zeros((4, 8, KH))
    twiddle[0], twiddle[1] = (t / math.sqrt(H) for t in wave(np.arange(HL), freq, H))
    twiddle[2, :TL], twiddle[3, :TL] = wave(np.arange(TL), freq, GH)
    return out + [twiddle.astype(np.float32)]


def halves(value):
    high = value.astype(jnp.bfloat16)
    return high, (value - high.astype(jnp.float32)).astype(jnp.bfloat16)


def dot3(a, b, dims):
    def one(x, y):
        return lax.dot_general(x, y, dims, preferred_element_type=jnp.float32)

    return one(a[0], b[1]) + one(a[1], b[0]) + one(a[0], b[0])


def gelu_slope(values):
    cdf = 0.5 * (1.0 + lax.erf(values * (1.0 / math.sqrt(2.0))))
    pdf = jnp.exp(-0.5 * values * values) * (1.0 / math.sqrt(2.0 * math.pi))
    return cdf + values * pdf


def kernel(
    field_hbm, weights_hbm, cot_hbm, fine_h, fine_l, coarse_h, coarse_l, ahead_h, ahead_l, behind_h, behind_l, twiddle_hbm,
    left_h, left_l, t1h, t1l, gweights,
    field, weights, cot, t4h, t4l, wah, wal, wbh, wbl, twiddle,
    send1, recv1, send2, recv2, send3, recv3, send4, recv4,
    csend, crecv, mixed, part_r, part_i, back_r, back_i,
    in_sem, row_send, row_recv, chan_send, chan_recv,
):
    me = lax.axis_index("rows")
    mc = lax.axis_index("chan")
    core, low = lax.rem(mc, 2), mc // 2
    me_y, me_x, me_z = me // 16, lax.rem(me // 4, 4), 2 * lax.rem(me, 4) + low
    mate = {"chan": mc + 1 - 2 * core}

    def partner(offset):
        dy, dx, dz = offset
        z = lax.rem(me_z + dz, 8)
        return lax.rem(me_y + dy, 8) * 16 + lax.rem(me_x + dx, 4) * 4 + z // 2, lax.rem(z, 2)

    barrier = pltpu.get_barrier_semaphore()
    for offset in FAR_FIRST:
        r, z = partner(offset)
        pl.semaphore_signal(barrier, inc=1, device_id={"rows": r, "chan": 2 * z + core}, device_id_type=MESH)
    pl.semaphore_signal(barrier, inc=1, device_id=mate, device_id_type=MESH)

    loads = [
        pltpu.make_async_copy(src, dst, in_sem.at[n])
        for n, (src, dst) in enumerate(
            [
                (field_hbm, field), (fine_h, t1h), (fine_l, t1l), (ahead_h, wah), (ahead_l, wal), (twiddle_hbm, twiddle),
                (weights_hbm, weights), (behind_h, wbh), (behind_l, wbl), (coarse_h, t4h), (coarse_l, t4l), (cot_hbm, cot),
            ]
        )
    ]
    for load in loads:
        load.start()

    def spread_rows(send, recv, n):
        def copy(r, z, device, which):
            pltpu.make_async_remote_copy(
                src_ref=send.at[r, z], dst_ref=recv.at[me, low], send_sem=row_send.at[n, which],
                recv_sem=row_recv.at[n, which], device_id=device, device_id_type=MESH,
            ).start()

        same = lax.rem(low + 1, 2)
        for dy, dx, dz in FAR_FIRST:
            r, z = partner((dy, dx, dz))
            if (dy, dx) == (0, 0) and dz in (1, 7):
                continue
            copy(r, z, {"rows": r, "chan": 2 * z + core}, 0)
        other = lax.rem(me_z + 7 + 2 * low, 8)
        r, z = me // 4 * 4 + other // 2, lax.rem(other, 2)
        copy(r, z, {"rows": r, "chan": 2 * z + core}, 0)
        copy(me, same, {"chan": 2 * same + core}, 1)
        recv[me, low] = send[me, low]

    def all_but_one(ref):
        return ref.at[pl.ds(0, ROWS - 1)]

    def await_rows(recv, n):
        part = all_but_one(recv)
        pltpu.make_async_copy(part, part, row_recv.at[n, 0]).wait()
        part = recv.at[me, lax.rem(low + 1, 2)]
        pltpu.make_async_copy(part, part, row_recv.at[n, 1]).wait()

    def await_sent(send, n):
        part = all_but_one(send)
        pltpu.make_async_copy(part, part, row_send.at[n, 0]).wait()
        part = send.at[me, lax.rem(low + 1, 2)]
        pltpu.make_async_copy(part, part, row_send.at[n, 1]).wait()

    def swap(n):
        return pltpu.make_async_remote_copy(
            src_ref=csend.at[n, 1 - core], dst_ref=crecv.at[n, core], send_sem=chan_send.at[n], recv_sem=chan_recv.at[n],
            device_id=mate, device_id_type=MESH,
        )

    def start_swap(n):
        swap(n).start()
        crecv[n, core] = csend[n, core]

    def to_modes(rows, steps, table, n):
        product = dot3(halves(rows), (wah[...], wal[...]), NN)
        for z in range(2):
            for j in range(2):
                lanes = slice(128 * j, 128 * j + 128)
                real = imag = None
                for l in range(steps):
                    first = 16 * (steps * z + l)
                    re, im = product[first : first + 16, :128], product[first : first + 16, 128:]
                    c, s = twiddle[table, l : l + 1, lanes], twiddle[table + 1, l : l + 1, lanes]
                    more_r, more_i = c * re + s * im, c * im - s * re
                    real, imag = (more_r, more_i) if l == 0 else (real + more_r, imag + more_i)
                csend[n, j, z, 0:16, :] = real
                csend[n, j, z, 16:32, :] = imag
        start_swap(n)

    def from_modes(n, steps, table):
        rows = []
        for z in range(2):
            for l in range(steps):
                real = imag = 0.0
                for j in range(2):
                    lanes = slice(128 * j, 128 * j + 128)
                    re, im = crecv[n, j, z, 0:16, :], crecv[n, j, z, 16:32, :]
                    c, s = twiddle[table, l : l + 1, lanes], twiddle[table + 1, l : l + 1, lanes]
                    real, imag = real + (c * re - s * im), imag + (s * re + c * im)
                rows.append(jnp.concatenate([real, -imag], axis=1))
                rows.append(jnp.concatenate([imag, real], axis=1))
        return dot3((wbh[...], wbl[...]), halves(jnp.concatenate(rows, axis=0)), NT)

    def give_modes(n, real, imag):
        for z in range(2):
            for c in range(2):
                first = 16 * (2 * z + c)
                csend[n, c, z, 0:16, :] = real[first : first + 16, :]
                csend[n, c, z, 16:32, :] = imag[first : first + 16, :]
        start_swap(n)

    for n in (0, 1, 2):
        loads[n].wait()
    lines = jnp.concatenate([field[:, l, :] for l in range(HL)], axis=0)
    for k, folded in enumerate((lines[:, : W // 2] + lines[:, W // 2 :], lines[:, : W // 2] - lines[:, W // 2 :])):
        table = (t1h[256 * k : 256 * k + 256, :], t1l[256 * k : 256 * k + 256, :])
        spectra = dot3(table, halves(folded), NT)
        send1[:, k, 0, :] = spectra[:128]
        send1[:, k, 1, :] = spectra[128:]
    pl.semaphore_wait(barrier, 2 * ROWS)
    spread_rows(send1, recv1, 0)
    for n in range(3, 12):
        loads[n].wait()
    await_rows(recv1, 0)

    rows = [jnp.concatenate([recv1[:, z, 0, :].T, recv1[:, z, 1, :].T], axis=1) for z in range(2)]
    to_modes(jnp.concatenate(rows, axis=0), HL, 0, 0)

    def mix(ref, origin, z, carry):
        def step(i, carry):
            out_r, out_i = carry
            xr, xi = ref[0, origin, z, pl.ds(i, 1), :], ref[0, origin, z, pl.ds(16 + i, 1), :]
            channel = 32 * z + 16 * origin + i
            wr, wi = weights[0, channel].astype(jnp.float32), weights[1, channel].astype(jnp.float32)
            return out_r + (xr * wr - xi * wi), out_i + (xr * wi + xi * wr)

        return lax.fori_loop(0, 16, step, carry, unroll=4)

    zero = jnp.zeros((64, 128), jnp.float32)
    total = (zero, zero)
    for z in range(2):
        total = mix(csend, core, z, total)
    swap(0).wait_recv()
    for z in range(2):
        total = mix(crecv, 1 - core, z, total)
    give_modes(1, *total)
    swap(1).wait_recv()

    short = from_modes(1, TL, 2)
    for s in range(2):
        send2[:, s, 0, :] = short[:, 128 * s : 128 * s + 128]
    spread_rows(send2, recv2, 1)
    await_rows(recv2, 1)
    turns = [recv2[:, k, 0, :].T for k in range(2)]
    parts = []
    for k in range(2):
        rows = []
        for t in range(TL):
            rows.append(jnp.concatenate([turns[k][32 * t : 32 * t + 16], turns[k][32 * t + 16 : 32 * t + 32]], axis=1))
        table = (t4h[256 * k : 256 * k + 256, :], t4l[256 * k : 256 * k + 256, :])
        parts.append(dot3(halves(jnp.concatenate(rows, axis=0)), table, NN))
    values = jnp.concatenate([parts[0] + parts[1], parts[0] - parts[1]], axis=1)
    cotangent = jnp.concatenate([cot[:, t, :] for t in range(TL)], axis=0)
    grad_v = cotangent * gelu_slope(values)

    for k, folded in enumerate((grad_v[:, :256] + grad_v[:, 256:], grad_v[:, :256] - grad_v[:, 256:])):
        table = (t4h[256 * k : 256 * k + 256, :], t4l[256 * k : 256 * k + 256, :])
        cols = dot3(table, halves(folded), NT)
        send3[:, k, 0, :] = jnp.concatenate([cols[:128], cols[128:]], axis=1)
    spread_rows(send3, recv3, 2)
    await_rows(recv3, 2)
    turns = [recv3[:, z, 0, :].T for z in range(2)]
    rows = [jnp.concatenate([turn[:64], turn[64:]], axis=1) for turn in turns]
    to_modes(jnp.concatenate(rows, axis=0), TL, 2, 2)

    def terms(ref, origin, i):
        real = imag = 0.0
        for z in range(2):
            gr, gi = ref[2, origin, z, 0:16, :], ref[2, origin, z, 16:32, :]
            own = pl.ds(pl.multiple_of(32 * z + 16 * origin, 16), 16)
            wr, wi = weights[0, i, own, :].astype(jnp.float32), weights[1, i, own, :].astype(jnp.float32)
            real, imag = real + (wr * gr + wi * gi), imag + (wr * gi - wi * gr)
        return real[:8] + real[8:], imag[:8] + imag[8:]

    def unmix_own(i, _):
        part_r[i], part_i[i] = terms(csend, core, i)
        return 0

    def unmix(i, _):
        real, imag = terms(crecv, 1 - core, i)
        back_r[pl.ds(i, 1), :] = jnp.sum(part_r[i] + real, axis=0, keepdims=True)
        back_i[pl.ds(i, 1), :] = jnp.sum(part_i[i] + imag, axis=0, keepdims=True)
        return 0

    lax.fori_loop(0, 64, unmix_own, 0, unroll=4)
    swap(2).wait_recv()
    lax.fori_loop(0, 64, unmix, 0, unroll=4)
    give_modes(3, back_r, back_i)
    swap(3).wait_recv()

    tall = from_modes(3, HL, 0)
    for s in range(4):
        send4[:, s // 2, s % 2, :] = tall[:, 128 * s : 128 * s + 128]
    spread_rows(send4, recv4, 3)

    def outer(i, _):
        z, origin, c = i // 32, lax.rem(i // 16, 2), lax.rem(i, 16)
        xr, xi = crecv[0, origin, z, pl.ds(c, 1), :], crecv[0, origin, z, pl.ds(16 + c, 1), :]
        for o in range(CHANS):
            gr, gi = crecv[2, o % 2, o // 2, 0:16, :], crecv[2, o % 2, o // 2, 16:32, :]
            gweights[0, i, 16 * o : 16 * o + 16, :] = (xr * gr + xi * gi).astype(jnp.bfloat16)
            gweights[1, i, 16 * o : 16 * o + 16, :] = (xr * gi - xi * gr).astype(jnp.bfloat16)
        return 0

    lax.fori_loop(0, 64, outer, 0, unroll=4)
    for n, send in enumerate((send1, send2, send3)):
        await_sent(send, n)
    for n in range(4):
        swap(n).wait_send()
    await_rows(recv4, 3)
    for k in range(2):
        for s in range(2):
            turn = recv4[:, k, s, :].T
            for l in range(4):
                for p in range(2):
                    first = 32 * l + 16 * p
                    mixed[2 * k + p, pl.ds(4 * s + l, 16, stride=HL), :] = turn[first : first + 16]
    for k in range(2):
        high, low_half = halves(jnp.concatenate([mixed[2 * k], mixed[2 * k + 1]], axis=1))
        left_h[128 * k : 128 * k + 128, :] = high
        left_l[128 * k : 128 * k + 128, :] = low_half
    await_sent(send4, 3)


def finish(left_h, left_l, t1h, t1l, gweights, gfield, gweights_hbm, sem):
    stores = []
    for n in range(8):
        part = (n // 4, pl.ds(n % 4 * 16, 16))
        stores.append(pltpu.make_async_copy(gweights.at[part], gweights_hbm.at[part], sem.at[n]))
        stores[-1].start()
    parts = []
    for k in range(2):
        lines, table = slice(128 * k, 128 * k + 128), slice(256 * k, 256 * k + 256)
        parts.append(dot3((left_h[lines, :], left_l[lines, :]), (t1h[table, :], t1l[table, :]), NN))
    whole = jnp.concatenate([parts[0] + parts[1], parts[0] - parts[1]], axis=1)
    gfield[...] = whole.reshape(gfield.shape).astype(jnp.bfloat16)
    for store in stores:
        store.wait()


def local(field, weights, cotangent):
    f32, bf16 = jnp.float32, jnp.bfloat16
    consts = [jnp.asarray(t) for t in tables()]
    anywhere = pl.BlockSpec(memory_space=pl.ANY)
    inside = pl.BlockSpec(memory_space=pltpu.VMEM)
    operands = [pltpu.with_memory_space_constraint(x, pltpu.HBM) for x in (field, weights, cotangent, *consts)]
    kept = pl.pallas_call(
        kernel,
        out_shape=(
            pltpu.VMEM((256, 256), bf16),
            pltpu.VMEM((256, 256), bf16),
            pltpu.VMEM(consts[0].shape, bf16),
            pltpu.VMEM(consts[1].shape, bf16),
            pltpu.VMEM(weights.shape, bf16),
        ),
        in_specs=[anywhere] * len(operands),
        out_specs=(inside,) * 5,
        scratch_shapes=[
            pltpu.VMEM(field.shape, f32),
            pltpu.VMEM(weights.shape, bf16),
            pltpu.VMEM(cotangent.shape, f32),
            *[pltpu.VMEM(t.shape, t.dtype) for t in consts[2:]],
            *[pltpu.VMEM((ROWS, 2, n, 128), f32) for n in (2, 2, 1, 1, 1, 1, 2, 2)],
            pltpu.VMEM((4, 2, 2, 32, 128), f32),
            pltpu.VMEM((4, 2, 2, 32, 128), f32),
            pltpu.VMEM((4, 128, 128), f32),
            *[pltpu.VMEM((64, 8, 128), f32)] * 2,
            *[pltpu.VMEM((64, 128), f32)] * 2,
            pltpu.SemaphoreType.DMA((12,)),
            pltpu.SemaphoreType.DMA((4, 2)),
            pltpu.SemaphoreType.DMA((4, 2)),
            pltpu.SemaphoreType.DMA((4,)),
            pltpu.SemaphoreType.DMA((4,)),
        ],
        compiler_params=pltpu.CompilerParams(
            collective_id=0, has_side_effects=True, vmem_limit_bytes=40 * 2**20
        ),
    )(*operands)
    return pl.pallas_call(
        finish,
        out_shape=(
            jax.ShapeDtypeStruct(field.shape, bf16),
            jax.ShapeDtypeStruct(weights.shape, bf16),
        ),
        in_specs=[inside] * 5,
        out_specs=(inside, anywhere),
        scratch_shapes=[pltpu.SemaphoreType.DMA((8,))],
        compiler_params=pltpu.CompilerParams(vmem_limit_bytes=16 * 2**20),
    )(*kept)


def solution(mesh):
    spread = P("chan", "rows", None)
    by_mode = P(None, None, None, ("rows", "chan"))
    return jax.shard_map(
        local, mesh=mesh, in_specs=(spread, by_mode, spread), out_specs=(spread, by_mode), check_vma=False
    )
```

```python
import math

import jax
import jax.numpy as jnp
import ml_dtypes
import numpy as np
from jax import lax
from jax.experimental import pallas as pl
from jax.experimental.pallas import tpu as pltpu
from jax.sharding import PartitionSpec as P

MESH = pl.DeviceIdType.MESH
ROWS = 128
CHANS = 4
KW = 256
KH = 256
W = 1024
H = 1024
GH = 512
GW = 512
HL = H // ROWS
TL = GH // ROWS
EIGHT = (4, 3, 5, 2, 6, 1, 7, 0)
FAR_FIRST = sorted(
    ((dy, dx, dz) for dx in (2, 1, 3, 0) for dz in EIGHT for dy in EIGHT if (dy, dx, dz) != (0, 0, 0)),
    key=lambda o: -(min(o[0], 8 - o[0]) + min(o[1], 4 - o[1]) + min(o[2], 8 - o[2])),
)
NT = (((1,), (1,)), ((), ()))
NN = (((1,), (0,)), ((), ()))


def split_table(table):
    high = table.astype(np.float32).astype(ml_dtypes.bfloat16)
    low = (table - high.astype(np.float64)).astype(np.float32).astype(ml_dtypes.bfloat16)
    return high, low


def wave(first, second, length):
    angle = (first[:, None] * second[None, :]) % length * (2.0 * math.pi / length)
    return np.cos(angle), np.sin(angle)


def tables():
    dev = np.arange(ROWS)
    freq = np.arange(KH) - KH // 2
    fine, coarse = [], []
    for k in range(2):
        c, s = wave(2 * dev + k, np.arange(W // 2), W)
        fine += [c / math.sqrt(W), -s / math.sqrt(W)]
        c, s = wave(2 * dev + k, np.arange(GW // 2), GW)
        coarse += [c / math.sqrt(KH * KW), -s / math.sqrt(KH * KW)]
    c, s = wave(dev, dev, ROWS)
    ahead = np.block([[c, -s], [s, c]])
    back = np.concatenate([c, s], 1)
    out = []
    for table in (np.concatenate(fine, 0), np.concatenate(coarse, 0), ahead, back):
        out += split_table(table)
    twiddle = np.zeros((4, 8, KH))
    twiddle[0], twiddle[1] = (t / math.sqrt(H) for t in wave(np.arange(HL), freq, H))
    twiddle[2, :TL], twiddle[3, :TL] = wave(np.arange(TL), freq, GH)
    return out + [twiddle.astype(np.float32)]


def halves(value):
    high = value.astype(jnp.bfloat16)
    return high, (value - high.astype(jnp.float32)).astype(jnp.bfloat16)


def dot3(a, b, dims):
    def one(x, y):
        return lax.dot_general(x, y, dims, preferred_element_type=jnp.float32)

    return one(a[0], b[1]) + one(a[1], b[0]) + one(a[0], b[0])


def gelu_slope(values):
    cdf = 0.5 * (1.0 + lax.erf(values * (1.0 / math.sqrt(2.0))))
    pdf = jnp.exp(-0.5 * values * values) * (1.0 / math.sqrt(2.0 * math.pi))
    return cdf + values * pdf


def kernel(
    field_hbm, weights_hbm, cot_hbm, fine_h, fine_l, coarse_h, coarse_l, ahead_h, ahead_l, behind_h, behind_l, twiddle_hbm,
    left_h, left_l, t1h, t1l, gweights,
    field, weights, cot, t4h, t4l, wah, wal, wbh, wbl, twiddle,
    send1, recv1, send2, recv2, send3, recv3, send4, recv4,
    csend, crecv, mixed, part_r, part_i, back_r, back_i,
    in_sem, row_send, row_recv, chan_send, chan_recv,
):
    me = lax.axis_index("rows")
    mc = lax.axis_index("chan")
    core, low = lax.rem(mc, 2), mc // 2
    me_y, me_x, me_z = me // 16, lax.rem(me // 4, 4), 2 * lax.rem(me, 4) + low
    mate = {"chan": mc + 1 - 2 * core}

    at_yx = [[lax.rem(me_y + dy, 8) * 32 + lax.rem(me_x + dx, 4) * 8 for dx in range(4)] for dy in range(8)]
    at_z = [lax.rem(me_z + dz, 8) for dz in range(8)]
    own = 2 * me + low
    partners = [at_yx[dy][dx] + at_z[dz] for dy, dx, dz in FAR_FIRST]

    barrier = pltpu.get_barrier_semaphore()
    for d in partners:
        pl.semaphore_signal(barrier, inc=1, device_id=2 * d + core, device_id_type=pl.DeviceIdType.LOGICAL)
    pl.semaphore_signal(barrier, inc=1, device_id=mate, device_id_type=MESH)

    loads = [
        pltpu.make_async_copy(src, dst, in_sem.at[n])
        for n, (src, dst) in enumerate(
            [
                (field_hbm, field), (fine_h, t1h), (fine_l, t1l), (ahead_h, wah), (ahead_l, wal), (twiddle_hbm, twiddle),
                (weights_hbm, weights), (behind_h, wbh), (behind_l, wbl), (coarse_h, t4h), (coarse_l, t4l), (cot_hbm, cot),
            ]
        )
    ]
    for load in loads:
        load.start()

    def spread_rows(send, recv, n):
        source, target = flat(send), flat(recv)
        for d in partners:
            pltpu.make_async_remote_copy(
                src_ref=source.at[d], dst_ref=target.at[own], send_sem=row_send.at[n], recv_sem=row_recv.at[n],
                device_id=2 * d + core, device_id_type=pl.DeviceIdType.LOGICAL,
            ).start()
        recv[me, low] = send[me, low]

    def flat(ref):
        return ref.reshape(2 * ROWS, *ref.shape[2:])

    def all_but_one(ref):
        return flat(ref).at[pl.ds(0, 2 * ROWS - 1)]

    def await_rows(recv, n):
        part = all_but_one(recv)
        pltpu.make_async_copy(part, part, row_recv.at[n]).wait()

    def await_sent(send, n):
        part = all_but_one(send)
        pltpu.make_async_copy(part, part, row_send.at[n]).wait()

    def swap(n):
        return pltpu.make_async_remote_copy(
            src_ref=csend.at[n, 1 - core], dst_ref=crecv.at[n, core], send_sem=chan_send.at[n], recv_sem=chan_recv.at[n],
            device_id=mate, device_id_type=MESH,
        )

    def start_swap(n):
        swap(n).start()
        crecv[n, core] = csend[n, core]

    def to_modes(rows, steps, table, n):
        product = dot3(halves(rows), (wah[...], wal[...]), NN)
        for z in range(2):
            for j in range(2):
                lanes = slice(128 * j, 128 * j + 128)
                real = imag = None
                for l in range(steps):
                    first = 16 * (steps * z + l)
                    re, im = product[first : first + 16, :128], product[first : first + 16, 128:]
                    c, s = twiddle[table, l : l + 1, lanes], twiddle[table + 1, l : l + 1, lanes]
                    more_r, more_i = c * re + s * im, c * im - s * re
                    real, imag = (more_r, more_i) if l == 0 else (real + more_r, imag + more_i)
                csend[n, j, z, 0:16, :] = real
                csend[n, j, z, 16:32, :] = imag
        start_swap(n)

    def from_modes(n, steps, table):
        rows = []
        for z in range(2):
            for l in range(steps):
                real = imag = 0.0
                for j in range(2):
                    lanes = slice(128 * j, 128 * j + 128)
                    re, im = crecv[n, j, z, 0:16, :], crecv[n, j, z, 16:32, :]
                    c, s = twiddle[table, l : l + 1, lanes], twiddle[table + 1, l : l + 1, lanes]
                    real, imag = real + (c * re - s * im), imag + (s * re + c * im)
                rows.append(jnp.concatenate([real, -imag], axis=1))
                rows.append(jnp.concatenate([imag, real], axis=1))
        return dot3((wbh[...], wbl[...]), halves(jnp.concatenate(rows, axis=0)), NT)

    def give_modes(n, real, imag):
        for z in range(2):
            for c in range(2):
                first = 16 * (2 * z + c)
                csend[n, c, z, 0:16, :] = real[first : first + 16, :]
                csend[n, c, z, 16:32, :] = imag[first : first + 16, :]
        start_swap(n)

    for n in (0, 1, 2):
        loads[n].wait()
    lines = jnp.concatenate([field[:, l, :] for l in range(HL)], axis=0)
    for k, folded in enumerate((lines[:, : W // 2] + lines[:, W // 2 :], lines[:, : W // 2] - lines[:, W // 2 :])):
        table = (t1h[256 * k : 256 * k + 256, :], t1l[256 * k : 256 * k + 256, :])
        spectra = dot3(table, halves(folded), NT)
        send1[:, k, 0, :] = spectra[:128]
        send1[:, k, 1, :] = spectra[128:]
    pl.semaphore_wait(barrier, 2 * ROWS)
    spread_rows(send1, recv1, 0)
    for n in range(3, 12):
        loads[n].wait()
    await_rows(recv1, 0)

    rows = [jnp.concatenate([recv1[:, z, 0, :].T, recv1[:, z, 1, :].T], axis=1) for z in range(2)]
    to_modes(jnp.concatenate(rows, axis=0), HL, 0, 0)

    def mix(ref, origin, z, carry):
        def step(i, carry):
            out_r, out_i = carry
            xr, xi = ref[0, origin, z, pl.ds(i, 1), :], ref[0, origin, z, pl.ds(16 + i, 1), :]
            channel = 32 * z + 16 * origin + i
            wr, wi = weights[0, channel].astype(jnp.float32), weights[1, channel].astype(jnp.float32)
            return out_r + (xr * wr - xi * wi), out_i + (xr * wi + xi * wr)

        return lax.fori_loop(0, 16, step, carry, unroll=4)

    zero = jnp.zeros((64, 128), jnp.float32)
    total = (zero, zero)
    for z in range(2):
        total = mix(csend, core, z, total)
    swap(0).wait_recv()
    for z in range(2):
        total = mix(crecv, 1 - core, z, total)
    give_modes(1, *total)
    swap(1).wait_recv()

    short = from_modes(1, TL, 2)
    for s in range(2):
        send2[:, s, 0, :] = short[:, 128 * s : 128 * s + 128]
    spread_rows(send2, recv2, 1)
    await_rows(recv2, 1)
    turns = [recv2[:, k, 0, :].T for k in range(2)]
    parts = []
    for k in range(2):
        rows = []
        for t in range(TL):
            rows.append(jnp.concatenate([turns[k][32 * t : 32 * t + 16], turns[k][32 * t + 16 : 32 * t + 32]], axis=1))
        table = (t4h[256 * k : 256 * k + 256, :], t4l[256 * k : 256 * k + 256, :])
        parts.append(dot3(halves(jnp.concatenate(rows, axis=0)), table, NN))
    values = jnp.concatenate([parts[0] + parts[1], parts[0] - parts[1]], axis=1)
    cotangent = jnp.concatenate([cot[:, t, :] for t in range(TL)], axis=0)
    grad_v = cotangent * gelu_slope(values)

    for k, folded in enumerate((grad_v[:, :256] + grad_v[:, 256:], grad_v[:, :256] - grad_v[:, 256:])):
        table = (t4h[256 * k : 256 * k + 256, :], t4l[256 * k : 256 * k + 256, :])
        cols = dot3(table, halves(folded), NT)
        send3[:, k, 0, :] = jnp.concatenate([cols[:128], cols[128:]], axis=1)
    spread_rows(send3, recv3, 2)
    await_rows(recv3, 2)
    turns = [recv3[:, z, 0, :].T for z in range(2)]
    rows = [jnp.concatenate([turn[:64], turn[64:]], axis=1) for turn in turns]
    to_modes(jnp.concatenate(rows, axis=0), TL, 2, 2)

    def terms(ref, origin, i):
        real = imag = 0.0
        for z in range(2):
            gr, gi = ref[2, origin, z, 0:16, :], ref[2, origin, z, 16:32, :]
            own = pl.ds(pl.multiple_of(32 * z + 16 * origin, 16), 16)
            wr, wi = weights[0, i, own, :].astype(jnp.float32), weights[1, i, own, :].astype(jnp.float32)
            real, imag = real + (wr * gr + wi * gi), imag + (wr * gi - wi * gr)
        return real[:8] + real[8:], imag[:8] + imag[8:]

    def unmix_own(i, _):
        part_r[i], part_i[i] = terms(csend, core, i)
        return 0

    def unmix(i, _):
        real, imag = terms(crecv, 1 - core, i)
        back_r[pl.ds(i, 1), :] = jnp.sum(part_r[i] + real, axis=0, keepdims=True)
        back_i[pl.ds(i, 1), :] = jnp.sum(part_i[i] + imag, axis=0, keepdims=True)
        return 0

    lax.fori_loop(0, 64, unmix_own, 0, unroll=4)
    swap(2).wait_recv()
    lax.fori_loop(0, 64, unmix, 0, unroll=4)
    give_modes(3, back_r, back_i)
    swap(3).wait_recv()

    tall = from_modes(3, HL, 0)
    for s in range(4):
        send4[:, s // 2, s % 2, :] = tall[:, 128 * s : 128 * s + 128]
    spread_rows(send4, recv4, 3)

    def outer(i, _):
        z, origin, c = i // 32, lax.rem(i // 16, 2), lax.rem(i, 16)
        xr, xi = crecv[0, origin, z, pl.ds(c, 1), :], crecv[0, origin, z, pl.ds(16 + c, 1), :]
        for o in range(CHANS):
            gr, gi = crecv[2, o % 2, o // 2, 0:16, :], crecv[2, o % 2, o // 2, 16:32, :]
            gweights[0, i, 16 * o : 16 * o + 16, :] = (xr * gr + xi * gi).astype(jnp.bfloat16)
            gweights[1, i, 16 * o : 16 * o + 16, :] = (xr * gi - xi * gr).astype(jnp.bfloat16)
        return 0

    lax.fori_loop(0, 64, outer, 0, unroll=4)
    for n, send in enumerate((send1, send2, send3)):
        await_sent(send, n)
    for n in range(4):
        swap(n).wait_send()
    await_rows(recv4, 3)
    for k in range(2):
        for s in range(2):
            turn = recv4[:, k, s, :].T
            for l in range(4):
                for p in range(2):
                    first = 32 * l + 16 * p
                    mixed[2 * k + p, pl.ds(4 * s + l, 16, stride=HL), :] = turn[first : first + 16]
    for k in range(2):
        high, low_half = halves(jnp.concatenate([mixed[2 * k], mixed[2 * k + 1]], axis=1))
        left_h[128 * k : 128 * k + 128, :] = high
        left_l[128 * k : 128 * k + 128, :] = low_half
    await_sent(send4, 3)


def finish(left_h, left_l, t1h, t1l, gweights, gfield_hbm, gweights_hbm, gfield, sem):
    stores = []
    for n in range(8):
        part = (n // 4, pl.ds(n % 4 * 16, 16))
        stores.append(pltpu.make_async_copy(gweights.at[part], gweights_hbm.at[part], sem.at[n]))
        stores[-1].start()
    parts = []
    for k in range(2):
        lines, table = slice(128 * k, 128 * k + 128), slice(256 * k, 256 * k + 256)
        parts.append(dot3((left_h[lines, :], left_l[lines, :]), (t1h[table, :], t1l[table, :]), NN))
    whole = jnp.concatenate([parts[0] + parts[1], parts[0] - parts[1]], axis=1)
    gfield[...] = whole.reshape(gfield.shape).astype(jnp.bfloat16)
    stores.append(pltpu.make_async_copy(gfield, gfield_hbm, sem.at[8]))
    stores[-1].start()
    for store in stores:
        store.wait()


def local(field, weights, cotangent):
    f32, bf16 = jnp.float32, jnp.bfloat16
    consts = [jnp.asarray(t) for t in tables()]
    anywhere = pl.BlockSpec(memory_space=pl.ANY)
    inside = pl.BlockSpec(memory_space=pltpu.VMEM)
    operands = [pltpu.with_memory_space_constraint(x, pltpu.HBM) for x in (field, weights, cotangent, *consts)]
    kept = pl.pallas_call(
        kernel,
        out_shape=(
            pltpu.VMEM((256, 256), bf16),
            pltpu.VMEM((256, 256), bf16),
            pltpu.VMEM(consts[0].shape, bf16),
            pltpu.VMEM(consts[1].shape, bf16),
            pltpu.VMEM(weights.shape, bf16),
        ),
        in_specs=[anywhere] * len(operands),
        out_specs=(inside,) * 5,
        scratch_shapes=[
            pltpu.VMEM(field.shape, f32),
            pltpu.VMEM(weights.shape, bf16),
            pltpu.VMEM(cotangent.shape, f32),
            *[pltpu.VMEM(t.shape, t.dtype) for t in consts[2:]],
            *[pltpu.VMEM((ROWS, 2, n, 128), f32) for n in (2, 2, 1, 1, 1, 1, 2, 2)],
            pltpu.VMEM((4, 2, 2, 32, 128), f32),
            pltpu.VMEM((4, 2, 2, 32, 128), f32),
            pltpu.VMEM((4, 128, 128), f32),
            *[pltpu.VMEM((64, 8, 128), f32)] * 2,
            *[pltpu.VMEM((64, 128), f32)] * 2,
            pltpu.SemaphoreType.DMA((12,)),
            pltpu.SemaphoreType.DMA((4,)),
            pltpu.SemaphoreType.DMA((4,)),
            pltpu.SemaphoreType.DMA((4,)),
            pltpu.SemaphoreType.DMA((4,)),
        ],
        compiler_params=pltpu.CompilerParams(
            collective_id=0, has_side_effects=True, vmem_limit_bytes=40 * 2**20
        ),
    )(*operands)
    return pl.pallas_call(
        finish,
        out_shape=(
            jax.ShapeDtypeStruct(field.shape, bf16),
            jax.ShapeDtypeStruct(weights.shape, bf16),
        ),
        in_specs=[inside] * 5,
        out_specs=(anywhere, anywhere),
        scratch_shapes=[pltpu.VMEM(field.shape, bf16), pltpu.SemaphoreType.DMA((9,))],
        compiler_params=pltpu.CompilerParams(vmem_limit_bytes=16 * 2**20),
    )(*kept)


def solution(mesh):
    spread = P("chan", "rows", None)
    by_mode = P(None, None, None, ("rows", "chan"))
    return jax.shard_map(
        local, mesh=mesh, in_specs=(spread, by_mode, spread), out_specs=(spread, by_mode), check_vma=False
    )
```

```python
import math

import jax
import jax.numpy as jnp
import ml_dtypes
import numpy as np
from jax import lax
from jax.experimental import pallas as pl
from jax.experimental.pallas import tpu as pltpu
from jax.sharding import PartitionSpec as P

MESH = pl.DeviceIdType.MESH
ROWS = 128
CHANS = 4
KW = 256
KH = 256
W = 1024
H = 1024
GH = 512
GW = 512
HL = H // ROWS
TL = GH // ROWS
EIGHT = (4, 3, 5, 2, 6, 1, 7, 0)
FAR_FIRST = sorted(
    ((dy, dx, dz) for dx in (2, 1, 3, 0) for dz in EIGHT for dy in EIGHT if (dy, dx, dz) != (0, 0, 0)),
    key=lambda o: -(min(o[0], 8 - o[0]) + min(o[1], 4 - o[1]) + min(o[2], 8 - o[2])),
)
NT = (((1,), (1,)), ((), ()))
NN = (((1,), (0,)), ((), ()))


def split_table(table):
    high = table.astype(np.float32).astype(ml_dtypes.bfloat16)
    low = (table - high.astype(np.float64)).astype(np.float32).astype(ml_dtypes.bfloat16)
    return high, low


def wave(first, second, length):
    angle = (first[:, None] * second[None, :]) % length * (2.0 * math.pi / length)
    return np.cos(angle), np.sin(angle)


def tables():
    dev = np.arange(ROWS)
    freq = np.arange(KH) - KH // 2
    fine, coarse = [], []
    for k in range(2):
        c, s = wave(2 * dev + k, np.arange(W // 2), W)
        fine += [c / math.sqrt(W), -s / math.sqrt(W)]
        c, s = wave(2 * dev + k, np.arange(GW // 2), GW)
        coarse += [c / math.sqrt(KH * KW), -s / math.sqrt(KH * KW)]
    c, s = wave(dev, dev, ROWS)
    ahead = np.block([[c, -s], [s, c]])
    back = np.concatenate([c, s], 1)
    out = []
    for table in (np.concatenate(fine, 0), np.concatenate(coarse, 0), ahead, back):
        out += split_table(table)
    twiddle = np.zeros((4, 8, KH))
    twiddle[0], twiddle[1] = (t / math.sqrt(H) for t in wave(np.arange(HL), freq, H))
    twiddle[2, :TL], twiddle[3, :TL] = wave(np.arange(TL), freq, GH)
    return out + [twiddle.astype(np.float32)]


def halves(value):
    high = value.astype(jnp.bfloat16)
    return high, (value - high.astype(jnp.float32)).astype(jnp.bfloat16)


def dot3(a, b, dims):
    def one(x, y):
        return lax.dot_general(x, y, dims, preferred_element_type=jnp.float32)

    return one(a[0], b[1]) + one(a[1], b[0]) + one(a[0], b[0])


def gelu_slope(values):
    cdf = 0.5 * (1.0 + lax.erf(values * (1.0 / math.sqrt(2.0))))
    pdf = jnp.exp(-0.5 * values * values) * (1.0 / math.sqrt(2.0 * math.pi))
    return cdf + values * pdf


def kernel(
    field_hbm, weights_hbm, cot_hbm, fine_h, fine_l, coarse_h, coarse_l, ahead_h, ahead_l, behind_h, behind_l, twiddle_hbm,
    left_h, left_l, t1h, t1l, gweights,
    field, weights, cot, t4h, t4l, wah, wal, wbh, wbl, twiddle,
    send1, recv1, send2, recv2, send3, recv3, send4, recv4,
    csend, crecv, mixed, part_r, part_i,
    in_sem, row_send, row_recv, chan_send, chan_recv,
):
    me = lax.axis_index("rows")
    mc = lax.axis_index("chan")
    core, low = lax.rem(mc, 2), mc // 2
    me_y, me_x, me_z = me // 16, lax.rem(me // 4, 4), 2 * lax.rem(me, 4) + low
    mate = {"chan": mc + 1 - 2 * core}

    at_yx = [[lax.rem(me_y + dy, 8) * 32 + lax.rem(me_x + dx, 4) * 8 for dx in range(4)] for dy in range(8)]
    at_z = [lax.rem(me_z + dz, 8) for dz in range(8)]
    own = 2 * me + low
    partners = [at_yx[dy][dx] + at_z[dz] for dy, dx, dz in FAR_FIRST]

    barrier = pltpu.get_barrier_semaphore()
    for d in partners:
        pl.semaphore_signal(barrier, inc=1, device_id=2 * d + core, device_id_type=pl.DeviceIdType.LOGICAL)
    pl.semaphore_signal(barrier, inc=1, device_id=mate, device_id_type=MESH)

    loads = [
        pltpu.make_async_copy(src, dst, in_sem.at[n])
        for n, (src, dst) in enumerate(
            [
                (field_hbm, field), (fine_h, t1h), (fine_l, t1l), (ahead_h, wah), (ahead_l, wal), (twiddle_hbm, twiddle),
                (weights_hbm, weights), (behind_h, wbh), (behind_l, wbl), (coarse_h, t4h), (coarse_l, t4l), (cot_hbm, cot),
            ]
        )
    ]
    for load in loads:
        load.start()

    def spread_rows(send, recv, n):
        source, target = flat(send), flat(recv)
        for d in partners:
            pltpu.make_async_remote_copy(
                src_ref=source.at[d], dst_ref=target.at[own], send_sem=row_send.at[n], recv_sem=row_recv.at[n],
                device_id=2 * d + core, device_id_type=pl.DeviceIdType.LOGICAL,
            ).start()
        recv[me, low] = send[me, low]

    def flat(ref):
        return ref.reshape(2 * ROWS, *ref.shape[2:])

    def all_but_one(ref):
        return flat(ref).at[pl.ds(0, 2 * ROWS - 1)]

    def await_rows(recv, n):
        part = all_but_one(recv)
        pltpu.make_async_copy(part, part, row_recv.at[n]).wait()

    def await_sent(send, n):
        part = all_but_one(send)
        pltpu.make_async_copy(part, part, row_send.at[n]).wait()

    def swap(n):
        return pltpu.make_async_remote_copy(
            src_ref=csend.at[n, 1 - core], dst_ref=crecv.at[n, core], send_sem=chan_send.at[n], recv_sem=chan_recv.at[n],
            device_id=mate, device_id_type=MESH,
        )

    def start_swap(n):
        swap(n).start()
        crecv[n, core] = csend[n, core]

    def to_modes(rows, steps, table, n):
        product = dot3(halves(rows), (wah[...], wal[...]), NN)
        for z in range(2):
            for j in range(2):
                lanes = slice(128 * j, 128 * j + 128)
                real = imag = None
                for l in range(steps):
                    first = 16 * (steps * z + l)
                    re, im = product[first : first + 16, :128], product[first : first + 16, 128:]
                    c, s = twiddle[table, l : l + 1, lanes], twiddle[table + 1, l : l + 1, lanes]
                    more_r, more_i = c * re + s * im, c * im - s * re
                    real, imag = (more_r, more_i) if l == 0 else (real + more_r, imag + more_i)
                csend[n, j, z, 0:16, :] = real
                csend[n, j, z, 16:32, :] = imag
        start_swap(n)

    def from_modes(n, steps, table):
        rows = []
        for z in range(2):
            for l in range(steps):
                real = imag = 0.0
                for j in range(2):
                    lanes = slice(128 * j, 128 * j + 128)
                    re, im = crecv[n, j, z, 0:16, :], crecv[n, j, z, 16:32, :]
                    c, s = twiddle[table, l : l + 1, lanes], twiddle[table + 1, l : l + 1, lanes]
                    real, imag = real + (c * re - s * im), imag + (s * re + c * im)
                rows.append(jnp.concatenate([real, -imag], axis=1))
                rows.append(jnp.concatenate([imag, real], axis=1))
        return dot3((wbh[...], wbl[...]), halves(jnp.concatenate(rows, axis=0)), NT)

    def give_modes(n, real, imag):
        for z in range(2):
            for c in range(2):
                first = 16 * (2 * z + c)
                csend[n, c, z, 0:16, :] = real[first : first + 16, :]
                csend[n, c, z, 16:32, :] = imag[first : first + 16, :]
        start_swap(n)

    for n in (0, 1, 2):
        loads[n].wait()
    lines = jnp.concatenate([field[:, l, :] for l in range(HL)], axis=0)
    for k, folded in enumerate((lines[:, : W // 2] + lines[:, W // 2 :], lines[:, : W // 2] - lines[:, W // 2 :])):
        table = (t1h[256 * k : 256 * k + 256, :], t1l[256 * k : 256 * k + 256, :])
        spectra = dot3(table, halves(folded), NT)
        send1[:, k, 0, :] = spectra[:128]
        send1[:, k, 1, :] = spectra[128:]
    pl.semaphore_wait(barrier, 2 * ROWS)
    spread_rows(send1, recv1, 0)
    for n in range(3, 12):
        loads[n].wait()
    await_rows(recv1, 0)

    rows = [jnp.concatenate([recv1[:, z, 0, :].T, recv1[:, z, 1, :].T], axis=1) for z in range(2)]
    to_modes(jnp.concatenate(rows, axis=0), HL, 0, 0)

    def mix(ref, origin, z, carry):
        def step(i, carry):
            out_r, out_i = carry
            xr, xi = ref[0, origin, z, pl.ds(i, 1), :], ref[0, origin, z, pl.ds(16 + i, 1), :]
            channel = 32 * z + 16 * origin + i
            wr, wi = weights[0, channel].astype(jnp.float32), weights[1, channel].astype(jnp.float32)
            return out_r + (xr * wr - xi * wi), out_i + (xr * wi + xi * wr)

        return lax.fori_loop(0, 16, step, carry, unroll=8)

    zero = jnp.zeros((64, 128), jnp.float32)
    total = (zero, zero)
    for z in range(2):
        total = mix(csend, core, z, total)
    swap(0).wait_recv()
    for z in range(2):
        total = mix(crecv, 1 - core, z, total)
    give_modes(1, *total)
    swap(1).wait_recv()

    short = from_modes(1, TL, 2)
    for s in range(2):
        send2[:, s, 0, :] = short[:, 128 * s : 128 * s + 128]
    spread_rows(send2, recv2, 1)
    await_rows(recv2, 1)
    turns = [recv2[:, k, 0, :].T for k in range(2)]
    parts = []
    for k in range(2):
        rows = []
        for t in range(TL):
            rows.append(jnp.concatenate([turns[k][32 * t : 32 * t + 16], turns[k][32 * t + 16 : 32 * t + 32]], axis=1))
        table = (t4h[256 * k : 256 * k + 256, :], t4l[256 * k : 256 * k + 256, :])
        parts.append(dot3(halves(jnp.concatenate(rows, axis=0)), table, NN))
    values = jnp.concatenate([parts[0] + parts[1], parts[0] - parts[1]], axis=1)
    cotangent = jnp.concatenate([cot[:, t, :] for t in range(TL)], axis=0)
    grad_v = cotangent * gelu_slope(values)

    for k, folded in enumerate((grad_v[:, :256] + grad_v[:, 256:], grad_v[:, :256] - grad_v[:, 256:])):
        table = (t4h[256 * k : 256 * k + 256, :], t4l[256 * k : 256 * k + 256, :])
        cols = dot3(table, halves(folded), NT)
        send3[:, k, 0, :] = jnp.concatenate([cols[:128], cols[128:]], axis=1)
    spread_rows(send3, recv3, 2)
    await_rows(recv3, 2)
    turns = [recv3[:, z, 0, :].T for z in range(2)]
    rows = [jnp.concatenate([turn[:64], turn[64:]], axis=1) for turn in turns]
    to_modes(jnp.concatenate(rows, axis=0), TL, 2, 2)

    def terms(ref, origin, i):
        real = imag = 0.0
        for z in range(2):
            gr, gi = ref[2, origin, z, 0:16, :], ref[2, origin, z, 16:32, :]
            own = pl.ds(pl.multiple_of(32 * z + 16 * origin, 16), 16)
            wr, wi = weights[0, i, own, :].astype(jnp.float32), weights[1, i, own, :].astype(jnp.float32)
            real, imag = real + (wr * gr + wi * gi), imag + (wr * gi - wi * gr)
        return real[:8] + real[8:], imag[:8] + imag[8:]

    def unmix_own(i, _):
        part_r[i], part_i[i] = terms(csend, core, i)
        return 0

    def unmix(i, _):
        real, imag = terms(crecv, 1 - core, i)
        part_r[i], part_i[i] = part_r[i] + real, part_i[i] + imag
        return 0

    lax.fori_loop(0, 64, unmix_own, 0, unroll=8)
    swap(2).wait_recv()
    lax.fori_loop(0, 64, unmix, 0, unroll=8)
    give_modes(3, *(sum(part[:, u, :] for u in range(8)) for part in (part_r, part_i)))
    swap(3).wait_recv()

    tall = from_modes(3, HL, 0)
    for s in range(4):
        send4[:, s // 2, s % 2, :] = tall[:, 128 * s : 128 * s + 128]
    spread_rows(send4, recv4, 3)

    def outer(i, _):
        z, origin, c = i // 32, lax.rem(i // 16, 2), lax.rem(i, 16)
        xr, xi = crecv[0, origin, z, pl.ds(c, 1), :], crecv[0, origin, z, pl.ds(16 + c, 1), :]
        for o in range(CHANS):
            gr, gi = crecv[2, o % 2, o // 2, 0:16, :], crecv[2, o % 2, o // 2, 16:32, :]
            gweights[0, i, 16 * o : 16 * o + 16, :] = (xr * gr + xi * gi).astype(jnp.bfloat16)
            gweights[1, i, 16 * o : 16 * o + 16, :] = (xr * gi - xi * gr).astype(jnp.bfloat16)
        return 0

    lax.fori_loop(0, 64, outer, 0, unroll=4)
    for n, send in enumerate((send1, send2, send3)):
        await_sent(send, n)
    for n in range(4):
        swap(n).wait_send()
    await_rows(recv4, 3)
    for k in range(2):
        for s in range(2):
            turn = recv4[:, k, s, :].T
            for l in range(4):
                for p in range(2):
                    first = 32 * l + 16 * p
                    mixed[2 * k + p, pl.ds(4 * s + l, 16, stride=HL), :] = turn[first : first + 16]
    for k in range(2):
        high, low_half = halves(jnp.concatenate([mixed[2 * k], mixed[2 * k + 1]], axis=1))
        left_h[128 * k : 128 * k + 128, :] = high
        left_l[128 * k : 128 * k + 128, :] = low_half
    await_sent(send4, 3)


def finish(left_h, left_l, t1h, t1l, gweights, gfield_hbm, gweights_hbm, gfield, sem):
    stores = []
    for n in range(8):
        part = (n // 4, pl.ds(n % 4 * 16, 16))
        stores.append(pltpu.make_async_copy(gweights.at[part], gweights_hbm.at[part], sem.at[n]))
        stores[-1].start()
    parts = []
    for k in range(2):
        lines, table = slice(128 * k, 128 * k + 128), slice(256 * k, 256 * k + 256)
        parts.append(dot3((left_h[lines, :], left_l[lines, :]), (t1h[table, :], t1l[table, :]), NN))
    whole = jnp.concatenate([parts[0] + parts[1], parts[0] - parts[1]], axis=1)
    gfield[...] = whole.reshape(gfield.shape).astype(jnp.bfloat16)
    stores.append(pltpu.make_async_copy(gfield, gfield_hbm, sem.at[8]))
    stores[-1].start()
    for store in stores:
        store.wait()


def local(field, weights, cotangent):
    f32, bf16 = jnp.float32, jnp.bfloat16
    consts = [jnp.asarray(t) for t in tables()]
    anywhere = pl.BlockSpec(memory_space=pl.ANY)
    inside = pl.BlockSpec(memory_space=pltpu.VMEM)
    operands = [pltpu.with_memory_space_constraint(x, pltpu.HBM) for x in (field, weights, cotangent, *consts)]
    kept = pl.pallas_call(
        kernel,
        out_shape=(
            pltpu.VMEM((256, 256), bf16),
            pltpu.VMEM((256, 256), bf16),
            pltpu.VMEM(consts[0].shape, bf16),
            pltpu.VMEM(consts[1].shape, bf16),
            pltpu.VMEM(weights.shape, bf16),
        ),
        in_specs=[anywhere] * len(operands),
        out_specs=(inside,) * 5,
        scratch_shapes=[
            pltpu.VMEM(field.shape, f32),
            pltpu.VMEM(weights.shape, bf16),
            pltpu.VMEM(cotangent.shape, f32),
            *[pltpu.VMEM(t.shape, t.dtype) for t in consts[2:]],
            *[pltpu.VMEM((ROWS, 2, n, 128), f32) for n in (2, 2, 1, 1, 1, 1, 2, 2)],
            pltpu.VMEM((4, 2, 2, 32, 128), f32),
            pltpu.VMEM((4, 2, 2, 32, 128), f32),
            pltpu.VMEM((4, 128, 128), f32),
            *[pltpu.VMEM((64, 8, 128), f32)] * 2,
            pltpu.SemaphoreType.DMA((12,)),
            pltpu.SemaphoreType.DMA((4,)),
            pltpu.SemaphoreType.DMA((4,)),
            pltpu.SemaphoreType.DMA((4,)),
            pltpu.SemaphoreType.DMA((4,)),
        ],
        compiler_params=pltpu.CompilerParams(
            collective_id=0, has_side_effects=True, vmem_limit_bytes=40 * 2**20
        ),
    )(*operands)
    return pl.pallas_call(
        finish,
        out_shape=(
            jax.ShapeDtypeStruct(field.shape, bf16),
            jax.ShapeDtypeStruct(weights.shape, bf16),
        ),
        in_specs=[inside] * 5,
        out_specs=(anywhere, anywhere),
        scratch_shapes=[pltpu.VMEM(field.shape, bf16), pltpu.SemaphoreType.DMA((9,))],
        compiler_params=pltpu.CompilerParams(vmem_limit_bytes=16 * 2**20),
    )(*kept)


def solution(mesh):
    spread = P("chan", "rows", None)
    by_mode = P(None, None, None, ("rows", "chan"))
    return jax.shard_map(
        local, mesh=mesh, in_specs=(spread, by_mode, spread), out_specs=(spread, by_mode), check_vma=False
    )
```
